768 devices in a mesh: gx: 4 (over x), yz: 192 (over z, y, core).
Axes of the slice: x: 4, y: 8, z: 12, core: 2. Of those that a mesh axis runs over, the one named last changes fastest.
Arguments:
- tokens: bfloat16 [384, 12288], P('yz', 'gx'), may hold values from -6 to 6
- counts: int32 [48], replicated, may hold values from 1 to 8, 192 in all
- gate_weight: bfloat16 [12288, 49152], P('gx', 'yz'), may hold values from -0.0546875 to 0.0546875
- up_weight: bfloat16 [12288, 49152], P('gx', 'yz'), may hold values from -0.0546875 to 0.0546875
- down_weight: bfloat16 [49152, 12288], P('yz', 'gx'), may hold values from -0.02734375 to 0.02734375
Outputs:
- mixed: bfloat16 [384, 12288], P('yz', 'gx')
The draws below stay inside these ranges and needn't reach their ends.
Inputs may be any that keep to these rules, and one draw needn't show every extreme that they name: `counts`: each group has 1 to 8 valid rows, its first ones; 192 valid rows in all; some group is full.
All inputs are finite; a program needn't handle non-finite values.
Results may differ from the reference program's by a relative error of at most 0.005.
Values may be sent and summed in bfloat16 or wider, within the bound.
No kernel may reach another device: no remote copies, remote signals or barrier semaphores. Data moves between devices by JAX's collectives and lax.ppermute only.
A program may use at most 32 MiB of HBM per device.

```python
import math
import jax
import jax.numpy as jnp
import numpy as np

D = 12288
FF = 49152
GROUP_ROWS = 8
ROWS = 384
GROUPS = 48
VALID = 192


def block_scale(stream_key, shape, split, smallest, largest):
    def one(axis_at, parts):
        draws = jax.random.uniform(jax.random.fold_in(jax.random.fold_in(stream_key, 6), axis_at), (parts,), jnp.float32, smallest / len(split), largest / len(split))
        return jnp.repeat(jnp.exp(draws), shape[axis_at] // parts).reshape((-1,) + (1,) * (len(shape) - axis_at - 1))

    gain = one(*split[0])
    for cut in split[1:]:
        gain = gain * one(*cut)
    return gain


def split_up(amount, total, limit, slope):
    portions = [(1 << 20) // math.isqrt(rank ** slope) + 1 for rank in range(2, amount + 1)]
    rest, given = total - limit - (amount - 1), [1] * (amount - 1)
    while rest > 0:
        free = [i for i in range(amount - 1) if given[i] < limit]
        mass, remaining = sum([portions[i] for i in free]), rest
        for i in free:
            extra = min(limit - given[i], max(1, remaining * portions[i] // mass), rest)
            given[i] = given[i] + extra
            rest = rest - extra
    return np.array([limit] + given)


def uneven(key, amount, total, bound, slope):
    if amount == 2:
        one = jax.random.randint(key, (), max(1, total - bound), min(bound, total - 1) + 1)
        return jnp.stack([one, total - one])
    lengths = jnp.asarray(split_up(amount, total, bound, slope), jnp.int32)
    pairs = (amount - 1) // 2
    giver, sink = lengths[1:1 + 2 * pairs:2], lengths[2:2 + 2 * pairs:2]
    room = jnp.minimum(giver - 1, bound - sink)
    moved = jax.random.randint(jax.random.fold_in(key, 1), (pairs,), 0, 1 << 20) % (room + 1)
    lengths = lengths.at[1:1 + 2 * pairs:2].set(giver - moved).at[2:2 + 2 * pairs:2].set(sink + moved)
    return lengths[jax.random.permutation(jax.random.fold_in(key, 2), amount)]


def bell_draw(rng, dims, deviation, reach, shards=(), kind=jnp.bfloat16):
    gain = block_scale(rng, dims, shards, -0.22, 0.18) if shards else 1.0
    values = jax.random.normal(rng, dims, jnp.float32) * deviation * gain
    return jnp.minimum(jnp.maximum(values, -reach), reach).astype(kind)


def setup_inputs(seed: int = 0) -> dict:
    streams_of = jax.random.split(jax.random.key(seed), 6)
    tokens = bell_draw(streams_of[0], (ROWS, D), 1.0, 6.0, ((0, 192), (1, 4)))
    counts = uneven(streams_of[1], GROUPS, VALID, GROUP_ROWS, 1).astype(jnp.int32)
    gate_weight = bell_draw(streams_of[2], (D, FF), D ** -0.5, 0.0546875, ((0, 4), (1, 192)))
    up_weight = bell_draw(streams_of[3], (D, FF), D ** -0.5, 0.0546875, ((0, 4), (1, 192)))
    down_weight = bell_draw(streams_of[4], (FF, D), FF ** -0.5, 0.02734375, ((0, 192), (1, 4)))
    return dict(tokens=tokens, counts=counts, gate_weight=gate_weight, up_weight=up_weight, down_weight=down_weight)


def reference(tokens, counts, gate_weight, up_weight, down_weight):
    row_ids = jnp.arange(ROWS, dtype=jnp.int32)
    groups = row_ids // GROUP_ROWS
    valid = (row_ids - groups * GROUP_ROWS) < counts[groups]
    masked = jnp.where(valid[:, None], tokens, jnp.zeros_like(tokens))
    gate = jnp.dot(masked, gate_weight, preferred_element_type=jnp.float32)
    up = jnp.dot(masked, up_weight, preferred_element_type=jnp.float32)
    hidden = (jax.nn.silu(gate) * up).astype(jnp.bfloat16)
    return jnp.dot(hidden, down_weight, preferred_element_type=jnp.float32).astype(jnp.bfloat16)
```

```python
import jax
import jax.numpy as jnp
from jax import lax
from jax.sharding import Mesh, PartitionSpec as P

GROUP_ROWS = 8
VALID = 192
Y = 8
C = 2
BF = jnp.bfloat16
F32 = jnp.float32


def exchange(x, axis):
    return lax.all_to_all(x, axis, split_axis=0, concat_axis=0, tiled=False)


def swap(x):
    return lax.ppermute(x, "c", [(0, 1), (1, 0)])


def places(counts, row_ids):
    n = counts.shape[0]
    before = jnp.sum(
        jnp.where(jnp.arange(n)[None, :] < jnp.arange(n)[:, None], counts[None, :], 0), axis=1
    )
    group = row_ids // GROUP_ROWS
    offset = row_ids - group * GROUP_ROWS
    hits = group[:, None] == jnp.arange(n, dtype=jnp.int32)[None, :]
    start = jnp.sum(jnp.where(hits, before[None, :], 0), axis=1)
    count = jnp.sum(jnp.where(hits, counts[None, :], 0), axis=1)
    return jnp.where(offset < count, start + offset, -1)


def shards(tokens, counts, gate_weight, up_weight, down_weight):
    rows, width = tokens.shape
    hidden_units = gate_weight.shape[1]
    gx, nz = lax.axis_size("gx"), lax.axis_size("z")
    total = nz * Y * C * rows
    core = lax.axis_index("c")

    by_z = exchange(jnp.broadcast_to(tokens[None], (nz, rows, width)), "z")
    by_z = by_z.reshape(nz * rows, width)
    own = exchange(jnp.broadcast_to(by_z[None], (Y, nz * rows, width)), "y")
    own = own.reshape(Y * nz * rows, width)
    other = swap(own)

    q = jnp.arange(Y * nz * rows, dtype=jnp.int32)
    base = (q // rows % nz) * (Y * C * rows) + (q // (rows * nz)) * (C * rows) + q % rows
    slots = jnp.arange(VALID, dtype=jnp.int32)[:, None]
    pick_own = (slots == places(counts, base + core * rows)[None, :]).astype(BF)
    pick_other = (slots == places(counts, base + (1 - core) * rows)[None, :]).astype(BF)
    x = (
        jnp.dot(pick_own, own, preferred_element_type=F32)
        + jnp.dot(pick_other, other, preferred_element_type=F32)
    ).astype(BF)

    part = hidden_units // gx
    gate = jnp.dot(x, gate_weight, preferred_element_type=F32).reshape(VALID, gx, part)
    up = jnp.dot(x, up_weight, preferred_element_type=F32).reshape(VALID, gx, part)
    both = jnp.concatenate((gate, up), axis=2).transpose(1, 0, 2)
    sums = jnp.sum(exchange(both, "gx"), axis=0)
    share = (jax.nn.silu(sums[:, :part]) * sums[:, part:]).astype(BF)
    hidden = lax.all_gather(share, "gx", axis=1, tiled=True)

    half = width // C
    w_own = lax.dynamic_slice_in_dim(down_weight, core * half, half, 1)
    w_other = lax.dynamic_slice_in_dim(down_weight, (1 - core) * half, half, 1)
    away = jnp.dot(hidden, w_other, preferred_element_type=F32).astype(BF)
    here = jnp.dot(hidden, w_own, preferred_element_type=F32)
    pair = here + swap(away).astype(F32)
    block = half // Y
    pieces = pair.astype(BF).reshape(VALID, Y, block).transpose(1, 0, 2)
    column = jnp.sum(exchange(pieces, "y").astype(F32), axis=0).astype(BF)

    everywhere = places(counts, jnp.arange(total, dtype=jnp.int32))
    spread = (everywhere[:, None] == jnp.arange(VALID, dtype=jnp.int32)[None, :]).astype(BF)
    padded = jnp.dot(spread, column, preferred_element_type=F32).astype(BF)
    padded = padded.reshape(nz, Y * C * rows, block)
    summed = jnp.sum(exchange(padded, "z").astype(F32), axis=0).astype(BF)
    mine = exchange(summed.reshape(Y * C, rows, block), ("y", "c"))
    mine = mine.reshape(Y, C, rows, block).transpose(2, 1, 0, 3)
    return mine.reshape(rows, width)


def solution(mesh):
    gx, yz = mesh.shape["gx"], mesh.shape["yz"]
    fine = Mesh(mesh.devices.reshape(gx, yz // (Y * C), Y, C), ("gx", "z", "y", "c"))
    line = ("z", "y", "c")
    placed = (P(line, "gx"), P(), P("gx", line), P("gx", line), P(line, "gx"))
    return jax.shard_map(
        shards, mesh=fine, in_specs=placed, out_specs=P(line, "gx"), check_vma=False
    )
```

```python
import jax
import jax.numpy as jnp
from jax import lax
from jax.sharding import Mesh, PartitionSpec as P

GROUP_ROWS = 8
VALID = 192
Y = 8
C = 2
BF = jnp.bfloat16
F32 = jnp.float32
SCALE = 32.0


def exchange(x, axis):
    return lax.all_to_all(x, axis, split_axis=0, concat_axis=0, tiled=False)


def swap(x):
    return lax.ppermute(x, "c", [(0, 1), (1, 0)])


def places(counts, row_ids):
    n = counts.shape[0]
    before = jnp.sum(
        jnp.where(jnp.arange(n)[None, :] < jnp.arange(n)[:, None], counts[None, :], 0), axis=1
    )
    group = row_ids // GROUP_ROWS
    offset = row_ids - group * GROUP_ROWS
    hits = group[:, None] == jnp.arange(n, dtype=jnp.int32)[None, :]
    start = jnp.sum(jnp.where(hits, before[None, :], 0), axis=1)
    count = jnp.sum(jnp.where(hits, counts[None, :], 0), axis=1)
    return jnp.where(offset < count, start + offset, -1)


def shards(tokens, counts, gate_weight, up_weight, down_weight):
    rows, width = tokens.shape
    hidden_units = gate_weight.shape[1]
    gx, nz = lax.axis_size("gx"), lax.axis_size("z")
    total = nz * Y * C * rows
    core = lax.axis_index("c")

    by_z = exchange(jnp.broadcast_to(tokens[None], (nz, rows, width)), "z")
    by_z = by_z.reshape(nz * rows, width)
    own = exchange(jnp.broadcast_to(by_z[None], (Y, nz * rows, width)), "y")
    own = own.reshape(Y * nz * rows, width)
    other = swap(own)

    q = jnp.arange(Y * nz * rows, dtype=jnp.int32)
    base = (q // rows % nz) * (Y * C * rows) + (q // (rows * nz)) * (C * rows) + q % rows
    slots = jnp.arange(VALID, dtype=jnp.int32)[:, None]
    pick_own = (slots == places(counts, base + core * rows)[None, :]).astype(BF)
    pick_other = (slots == places(counts, base + (1 - core) * rows)[None, :]).astype(BF)
    x = (
        jnp.dot(pick_own, own, preferred_element_type=F32)
        + jnp.dot(pick_other, other, preferred_element_type=F32)
    ).astype(BF)

    gate = jnp.dot(x, gate_weight, preferred_element_type=F32)
    up = jnp.dot(x, up_weight, preferred_element_type=F32)
    partial = (jnp.concatenate((gate, up), axis=1) * SCALE).astype(jnp.float16)
    parts = lax.all_gather(partial, "gx", axis=0, tiled=False)
    sums = jnp.sum(parts.astype(F32), axis=0) * (1.0 / SCALE)
    hidden = (jax.nn.silu(sums[:, :hidden_units]) * sums[:, hidden_units:]).astype(BF)

    half = width // C
    w_own = lax.dynamic_slice_in_dim(down_weight, core * half, half, 1)
    w_other = lax.dynamic_slice_in_dim(down_weight, (1 - core) * half, half, 1)
    away = jnp.dot(hidden, w_other, preferred_element_type=F32).astype(BF)
    here = jnp.dot(hidden, w_own, preferred_element_type=F32)
    pair = (here + swap(away).astype(F32)).astype(BF)

    tile = half // Y * 2 // 3
    tiles = pair.reshape(VALID, half // tile, tile).transpose(1, 0, 2)
    seconds = tiles[Y:].reshape(Y, VALID // 2, tile)
    pieces = jnp.concatenate((tiles[:Y], seconds), axis=1)
    column = jnp.sum(exchange(pieces, "y").astype(F32), axis=0).astype(BF)

    everywhere = places(counts, jnp.arange(total, dtype=jnp.int32))
    slots = jnp.arange(VALID, dtype=jnp.int32)
    spread = (everywhere[:, None] == slots[None, :]).astype(BF)
    first_slot = lax.axis_index("y") % 2 * (VALID // 2)
    spread_half = (everywhere[:, None] == first_slot + slots[None, : VALID // 2]).astype(BF)
    padded = jnp.concatenate(
        (
            jnp.dot(spread, column[:VALID], preferred_element_type=F32).astype(BF),
            jnp.dot(spread_half, column[VALID:], preferred_element_type=F32).astype(BF),
        ),
        axis=1,
    ).reshape(nz, Y * C * rows, 2 * tile)
    summed = jnp.sum(exchange(padded, "z").astype(F32), axis=0).astype(BF)
    mine = exchange(summed.reshape(Y * C, rows, 2 * tile), ("y", "c"))
    mine = mine.reshape(Y, C, rows, 2, tile)
    firsts = mine[:, :, :, 0].transpose(2, 1, 0, 3)
    pairs = mine[:, :, :, 1].reshape(Y // 2, 2, C, rows, tile)
    seconds = (pairs[:, 0] + pairs[:, 1]).transpose(2, 1, 0, 3)
    return jnp.concatenate((firsts, seconds), axis=2).reshape(rows, width)


def solution(mesh):
    gx, yz = mesh.shape["gx"], mesh.shape["yz"]
    fine = Mesh(mesh.devices.reshape(gx, yz // (Y * C), Y, C), ("gx", "z", "y", "c"))
    line = ("z", "y", "c")
    placed = (P(line, "gx"), P(), P("gx", line), P("gx", line), P(line, "gx"))
    return jax.shard_map(
        shards, mesh=fine, in_specs=placed, out_specs=P(line, "gx"), check_vma=False
    )
```

```python
import jax
import jax.numpy as jnp
from jax import lax
from jax.experimental import pallas as pl
from jax.experimental.pallas import tpu as pltpu
from jax.sharding import Mesh, PartitionSpec as P

GROUP_ROWS = 8
VALID = 192
Y = 8
C = 2
BF = jnp.bfloat16
F32 = jnp.float32
SCALE = 32.0
OVER_ROWS = (((0,), (0,)), ((), ()))


def exchange(x, axis):
    return lax.all_to_all(x, axis, split_axis=0, concat_axis=0, tiled=False)


def swap(x):
    return lax.ppermute(x, "c", [(0, 1), (1, 0)])


def places(counts, row_ids):
    n = counts.shape[0]
    before = jnp.sum(
        jnp.where(jnp.arange(n)[None, :] < jnp.arange(n)[:, None], counts[None, :], 0), axis=1
    )
    group = row_ids // GROUP_ROWS
    offset = row_ids - group * GROUP_ROWS
    hits = group[:, None] == jnp.arange(n, dtype=jnp.int32)[None, :]
    start = jnp.sum(jnp.where(hits, before[None, :], 0), axis=1)
    count = jnp.sum(jnp.where(hits, counts[None, :], 0), axis=1)
    return jnp.where(offset < count, start + offset, -1)


def gate_up(parity, blocks, gate_weight, up_weight):
    count, slots, block = blocks.shape
    units = gate_weight.shape[1]
    step = count // 2
    weight_shape = (count, C, block, units)

    def kernel(parity_ref, x_ref, gate_ref, up_ref, out_ref):
        gate = jnp.zeros((slots, units), F32)
        up = jnp.zeros((slots, units), F32)
        for i in range(step):
            gate += jnp.dot(x_ref[i], gate_ref[i, 0], preferred_element_type=F32)
            up += jnp.dot(x_ref[i], up_ref[i, 0], preferred_element_type=F32)

        @pl.when(pl.program_id(0) == 0)
        def _():
            out_ref[:, :units] = gate
            out_ref[:, units:] = up

        @pl.when(pl.program_id(0) > 0)
        def _():
            out_ref[:, :units] += gate
            out_ref[:, units:] += up

    weights = pl.BlockSpec((step, 1, block, units), lambda i, parity: (i, parity[0], 0, 0))
    return pl.pallas_call(
        kernel,
        out_shape=jax.ShapeDtypeStruct((slots, 2 * units), F32),
        grid_spec=pltpu.PrefetchScalarGridSpec(
            num_scalar_prefetch=1,
            grid=(count // step,),
            in_specs=[pl.BlockSpec((step, slots, block), lambda i, parity: (i, 0, 0)), weights, weights],
            out_specs=pl.BlockSpec((slots, 2 * units), lambda i, parity: (0, 0)),
        ),
        compiler_params=pltpu.CompilerParams(vmem_limit_bytes=32 << 20),
        cost_estimate=pl.CostEstimate(
            flops=4 * slots * count * block * units,
            bytes_accessed=4 * count * block * units,
            transcendentals=0,
        ),
    )(parity[None], blocks, gate_weight.reshape(weight_shape), up_weight.reshape(weight_shape))


def down(core, hidden, down_weight, got, tile):
    slots, units = hidden.shape
    half = got.shape[1]

    def kernel(core_ref, hidden_ref, weight_ref, got_ref, out_ref):
        pair = jnp.dot(hidden_ref[...], weight_ref[...], preferred_element_type=F32)
        pair = (pair + got_ref[...].astype(F32)).astype(BF)
        for i in range(half // tile):
            columns = pair[:, i * tile : (i + 1) * tile]
            if i < Y:
                out_ref[i, :slots] = columns
            else:
                j = 2 * (i - Y)
                out_ref[j, slots:] = columns[: slots // 2]
                out_ref[j + 1, slots:] = columns[slots // 2 :]

    return pl.pallas_call(
        kernel,
        out_shape=jax.ShapeDtypeStruct((Y, slots + slots // 2, tile), BF),
        grid_spec=pltpu.PrefetchScalarGridSpec(
            num_scalar_prefetch=1,
            grid=(1,),
            in_specs=[
                pl.BlockSpec((slots, units), lambda i, core: (0, 0)),
                pl.BlockSpec((units, half), lambda i, core: (0, core[0])),
                pl.BlockSpec((slots, half), lambda i, core: (0, 0)),
            ],
            out_specs=pl.BlockSpec((Y, slots + slots // 2, tile), lambda i, core: (0, 0, 0)),
        ),
        compiler_params=pltpu.CompilerParams(vmem_limit_bytes=32 << 20),
    )(core[None], hidden, down_weight, got)


def shards(tokens, counts, gate_weight, up_weight, down_weight):
    rows, width = tokens.shape
    hidden_units = gate_weight.shape[1]
    gx, nz = lax.axis_size("gx"), lax.axis_size("z")
    total = nz * Y * C * rows
    core = lax.axis_index("c")

    block = width // (Y * C)
    cut = tokens.reshape(rows, Y * C, block).transpose(1, 0, 2)
    near = exchange(cut, ("y", "c")).reshape(Y * C * rows, block)
    by_z = exchange(jnp.broadcast_to(near[None], (nz, Y * C * rows, block)), "z")
    by_z = by_z.reshape(total, block)

    everywhere = places(counts, jnp.arange(total, dtype=jnp.int32))
    slots = jnp.arange(VALID, dtype=jnp.int32)
    spread = (everywhere[:, None] == slots[None, :]).astype(BF)
    valid = lax.dot_general(spread, by_z, OVER_ROWS, preferred_element_type=F32)
    own = lax.all_gather(valid.astype(BF), "y", axis=0, tiled=False)
    other = swap(own)

    sum_own = gate_up(core, own, gate_weight, up_weight)
    sum_other = gate_up(1 - core, other, gate_weight, up_weight)
    partial = ((sum_own + sum_other) * SCALE).astype(jnp.float16)
    parts = lax.all_gather(partial, "gx", axis=0, tiled=False)
    sums = jnp.sum(parts.astype(F32), axis=0) * (1.0 / SCALE)
    hidden = (jax.nn.silu(sums[:, :hidden_units]) * sums[:, hidden_units:]).astype(BF)

    half = width // C
    w_other = lax.dynamic_slice_in_dim(down_weight, (1 - core) * half, half, 1)
    away = jnp.dot(hidden, w_other, preferred_element_type=F32).astype(BF)
    tile = half // Y * 2 // 3
    pieces = down(core, hidden, down_weight, swap(away), tile)
    column = jnp.sum(exchange(pieces, "y").astype(F32), axis=0).astype(BF)

    first_slot = lax.axis_index("y") % 2 * (VALID // 2)
    spread_half = (everywhere[:, None] == first_slot + slots[None, : VALID // 2]).astype(BF)
    padded = jnp.concatenate(
        (
            jnp.dot(spread, column[:VALID], preferred_element_type=F32).astype(BF),
            jnp.dot(spread_half, column[VALID:], preferred_element_type=F32).astype(BF),
        ),
        axis=1,
    ).reshape(nz, Y * C * rows, 2 * tile)
    summed = jnp.sum(exchange(padded, "z").astype(F32), axis=0).astype(BF)
    mine = exchange(summed.reshape(Y * C, rows, 2 * tile), ("y", "c"))
    mine = mine.reshape(Y, C, rows, 2, tile)
    firsts = mine[:, :, :, 0].transpose(2, 1, 0, 3)
    pairs = mine[:, :, :, 1].reshape(Y // 2, 2, C, rows, tile)
    seconds = (pairs[:, 0] + pairs[:, 1]).transpose(2, 1, 0, 3)
    return jnp.concatenate((firsts, seconds), axis=2).reshape(rows, width)


def solution(mesh):
    gx, yz = mesh.shape["gx"], mesh.shape["yz"]
    fine = Mesh(mesh.devices.reshape(gx, yz // (Y * C), Y, C), ("gx", "z", "y", "c"))
    line = ("z", "y", "c")
    placed = (P(line, "gx"), P(), P("gx", line), P("gx", line), P(line, "gx"))
    return jax.shard_map(
        shards, mesh=fine, in_specs=placed, out_specs=P(line, "gx"), check_vma=False
    )
```

```python
import jax
import jax.numpy as jnp
from jax import lax
from jax.experimental import pallas as pl
from jax.experimental.pallas import tpu as pltpu
from jax.sharding import Mesh, PartitionSpec as P

GROUP_ROWS = 8
VALID = 192
Y = 8
C = 2
BF = jnp.bfloat16
F32 = jnp.float32
SCALE = 32.0
OVER_ROWS = (((0,), (0,)), ((), ()))


def exchange(x, axis):
    return lax.all_to_all(x, axis, split_axis=0, concat_axis=0, tiled=False)


def swap(x):
    return lax.ppermute(x, "c", [(0, 1), (1, 0)])


def places(counts, row_ids):
    n = counts.shape[0]
    before = jnp.sum(
        jnp.where(jnp.arange(n)[None, :] < jnp.arange(n)[:, None], counts[None, :], 0), axis=1
    )
    group = row_ids // GROUP_ROWS
    offset = row_ids - group * GROUP_ROWS
    hits = group[:, None] == jnp.arange(n, dtype=jnp.int32)[None, :]
    start = jnp.sum(jnp.where(hits, before[None, :], 0), axis=1)
    count = jnp.sum(jnp.where(hits, counts[None, :], 0), axis=1)
    return jnp.where(offset < count, start + offset, -1)


def gate_up(kept, pick, other, gate_weight, up_weight):
    slots, width = kept.shape
    units = gate_weight.shape[1]
    steps = 4
    chunk = width // steps

    def kernel(kept_ref, pick_ref, other_ref, gate_ref, up_ref, out_ref):
        x = jnp.dot(pick_ref[...], other_ref[...], preferred_element_type=F32)
        x = (x + kept_ref[...].astype(F32)).astype(BF)
        gate = jnp.dot(x, gate_ref[...], preferred_element_type=F32) * SCALE
        up = jnp.dot(x, up_ref[...], preferred_element_type=F32) * SCALE

        @pl.when(pl.program_id(0) == 0)
        def _():
            out_ref[:, :units] = gate
            out_ref[:, units:] = up

        @pl.when(pl.program_id(0) > 0)
        def _():
            out_ref[:, :units] += gate
            out_ref[:, units:] += up

    def columns(rows):
        return pl.BlockSpec((rows, chunk), lambda i: (0, i))

    weights = pl.BlockSpec((chunk, units), lambda i: (i, 0))
    return pl.pallas_call(
        kernel,
        out_shape=jax.ShapeDtypeStruct((slots, 2 * units), F32),
        grid=(steps,),
        in_specs=[
            columns(slots),
            pl.BlockSpec(pick.shape, lambda i: (0, 0)),
            columns(other.shape[0]),
            weights,
            weights,
        ],
        out_specs=pl.BlockSpec((slots, 2 * units), lambda i: (0, 0)),
        compiler_params=pltpu.CompilerParams(vmem_limit_bytes=16 << 20),
    )(kept, pick, other, gate_weight, up_weight)


def shards(tokens, counts, gate_weight, up_weight, down_weight):
    rows, width = tokens.shape
    hidden_units = gate_weight.shape[1]
    nz = lax.axis_size("z")
    core = lax.axis_index("c")

    by_z = exchange(jnp.broadcast_to(tokens[None], (nz, rows, width)), "z")
    by_z = by_z.reshape(nz * rows, width)
    own = exchange(jnp.broadcast_to(by_z[None], (Y, nz * rows, width)), "y")
    own = own.reshape(Y * nz * rows, width)
    other = swap(own)

    q = jnp.arange(Y * nz * rows, dtype=jnp.int32)
    base = (q // rows % nz) * (Y * C * rows) + (q // (rows * nz)) * (C * rows) + q % rows
    slots = jnp.arange(VALID, dtype=jnp.int32)[:, None]
    pick_own = (slots == places(counts, base + core * rows)[None, :]).astype(BF)
    pick_other = (slots == places(counts, base + (1 - core) * rows)[None, :]).astype(BF)
    kept = jnp.dot(pick_own, own, preferred_element_type=F32).astype(BF)

    partial = gate_up(kept, pick_other, other, gate_weight, up_weight).astype(jnp.float16)
    parts = lax.all_gather(partial, "gx", axis=0, tiled=False)
    sums = jnp.sum(parts.astype(F32), axis=0) * (1.0 / SCALE)
    hidden = (jax.nn.silu(sums[:, :hidden_units]) * sums[:, hidden_units:]).astype(BF)

    mine = lax.dot_general(pick_own, hidden, OVER_ROWS, preferred_element_type=F32).astype(BF)
    theirs = lax.dot_general(pick_other, hidden, OVER_ROWS, preferred_element_type=F32).astype(BF)
    away = jnp.dot(theirs, down_weight, preferred_element_type=F32).astype(BF)
    here = jnp.dot(mine, down_weight, preferred_element_type=F32)
    pair = (here + swap(away).astype(F32)).astype(BF).reshape(Y, nz * rows, width)
    line = jnp.sum(exchange(pair, "y").astype(F32), axis=0).astype(BF).reshape(nz, rows, width)
    return jnp.sum(exchange(line, "z").astype(F32), axis=0).astype(BF)


def solution(mesh):
    gx, yz = mesh.shape["gx"], mesh.shape["yz"]
    fine = Mesh(mesh.devices.reshape(gx, yz // (Y * C), Y, C), ("gx", "z", "y", "c"))
    line = ("z", "y", "c")
    placed = (P(line, "gx"), P(), P("gx", line), P("gx", line), P(line, "gx"))
    return jax.shard_map(
        shards, mesh=fine, in_specs=placed, out_specs=P(line, "gx"), check_vma=False
    )
```

```python
import jax
import jax.numpy as jnp
from jax import lax
from jax.experimental import pallas as pl
from jax.experimental.pallas import tpu as pltpu
from jax.sharding import Mesh, PartitionSpec as P

GROUP_ROWS = 8
VALID = 192
Y = 8
C = 2
BF = jnp.bfloat16
F32 = jnp.float32
SCALE = 32.0
OVER_ROWS = (((0,), (0,)), ((), ()))


def exchange(x, axis):
    return lax.all_to_all(x, axis, split_axis=0, concat_axis=0, tiled=False)


def swap(x):
    return lax.ppermute(x, "c", [(0, 1), (1, 0)])


def one_hot(counts_ref, columns, shift):
    shape = (GROUP_ROWS, columns)
    row = lax.broadcasted_iota(jnp.int32, shape, 0)
    ahead = lax.broadcasted_iota(jnp.int32, shape, 1) - row
    start = -shift
    tiles = []
    for group in range(counts_ref.shape[0]):
        count = counts_ref[group]
        tiles.append(jnp.where((ahead == start) & (row < count), 1.0, 0.0))
        start += count
    return jnp.concatenate(tiles, axis=0).astype(BF)


def whole(shape):
    return pl.BlockSpec(shape, lambda *_: (0,) * len(shape))


def cut(tokens):
    rows, width = tokens.shape
    tile = width // (Y * C + Y)

    def kernel(in_ref, out_ref):
        for i in range(Y * C):
            second = Y * C + i // C
            out_ref[i, :, :tile] = in_ref[:, i * tile : (i + 1) * tile]
            out_ref[i, :, tile:] = in_ref[:, second * tile : (second + 1) * tile]

    return pl.pallas_call(
        kernel, out_shape=jax.ShapeDtypeStruct((Y * C, rows, 2 * tile), BF)
    )(tokens)


def compact(core, counts, padded):
    tile = padded.shape[1] // 2
    half = VALID // 2

    def kernel(core_ref, counts_ref, in_ref, out_ref):
        hot = one_hot(counts_ref, VALID, 0)
        x = lax.dot_general(hot, in_ref[...], OVER_ROWS, preferred_element_type=F32).astype(BF)
        first, second = x[:, :tile], x[:, tile:]
        for y in range(Y):
            out_ref[y, :VALID] = first

        @pl.when(core_ref[0] == 0)
        def _():
            for y in range(Y):
                out_ref[y, VALID:] = second[:half]

        @pl.when(core_ref[0] != 0)
        def _():
            for y in range(Y):
                out_ref[y, VALID:] = second[half:]

    shape = (Y, VALID + half, tile)
    return pl.pallas_call(
        kernel,
        out_shape=jax.ShapeDtypeStruct(shape, BF),
        grid_spec=pltpu.PrefetchScalarGridSpec(
            num_scalar_prefetch=2,
            grid=(1,),
            in_specs=[whole(padded.shape)],
            out_specs=whole(shape),
        ),
    )(core[None], counts, padded)


def spread(parity, counts, pieces):
    tile = pieces.shape[2]
    rows = counts.shape[0] * GROUP_ROWS
    half = VALID // 2

    def kernel(parity_ref, counts_ref, in_ref, out_ref):
        total = in_ref[0].astype(F32)
        for y in range(1, Y):
            total += in_ref[y].astype(F32)
        total = total.astype(BF)
        hot = one_hot(counts_ref, VALID, 0)
        hot_half = one_hot(counts_ref, half, parity_ref[0] * half)
        out_ref[:, :tile] = jnp.dot(hot, total[:VALID], preferred_element_type=F32).astype(BF)
        out_ref[:, tile:] = jnp.dot(hot_half, total[VALID:], preferred_element_type=F32).astype(BF)

    return pl.pallas_call(
        kernel,
        out_shape=jax.ShapeDtypeStruct((rows, 2 * tile), BF),
        grid_spec=pltpu.PrefetchScalarGridSpec(
            num_scalar_prefetch=2,
            grid=(1,),
            in_specs=[whole(pieces.shape)],
            out_specs=whole((rows, 2 * tile)),
        ),
    )(parity[None], counts, pieces)


def gate_up(core, own, other, gate_weight, up_weight):
    units = gate_weight.shape[1]
    tile = own.shape[2]
    steps = 3
    chunk = gate_weight.shape[0] // steps

    def kernel(core_ref, own_ref, other_ref, gate_ref, up_ref, out_ref):
        step = pl.program_id(0)
        first = core_ref[0] == 0

        def both(y):
            a, b = own_ref[y], other_ref[y]
            return jnp.where(first, a, b), jnp.where(first, b, a)

        def add(parts, start):
            gate = jnp.zeros((VALID, units), F32)
            up = jnp.zeros((VALID, units), F32)
            for i, x in enumerate(parts):
                depth = pl.ds(i * 2 * tile, 2 * tile)
                gate += jnp.dot(x, gate_ref[depth, :], preferred_element_type=F32)
                up += jnp.dot(x, up_ref[depth, :], preferred_element_type=F32)
            if start:
                out_ref[:, :units] = gate * SCALE
                out_ref[:, units:] = up * SCALE
            else:
                out_ref[:, :units] += gate * SCALE
                out_ref[:, units:] += up * SCALE

        def firsts(start):
            parts = []
            for y in range(start, start + Y // 2):
                a, b = both(y)
                parts.append(jnp.concatenate((a[:VALID], b[:VALID]), axis=1))
            return parts

        def seconds():
            parts = []
            for y in range(0, Y, 2):
                pair = [jnp.concatenate((a[VALID:], b[VALID:]), axis=0) for a, b in (both(y), both(y + 1))]
                parts.append(jnp.concatenate(pair, axis=1))
            return parts

        @pl.when(step == 0)
        def _():
            add(firsts(0), True)

        @pl.when(step == 1)
        def _():
            add(firsts(Y // 2), False)

        @pl.when(step == 2)
        def _():
            add(seconds(), False)

    weights = pl.BlockSpec((chunk, units), lambda i, core: (i, 0))
    return pl.pallas_call(
        kernel,
        out_shape=jax.ShapeDtypeStruct((VALID, 2 * units), F32),
        grid_spec=pltpu.PrefetchScalarGridSpec(
            num_scalar_prefetch=1,
            grid=(steps,),
            in_specs=[whole(own.shape), whole(own.shape), weights, weights],
            out_specs=whole((VALID, 2 * units)),
        ),
        compiler_params=pltpu.CompilerParams(vmem_limit_bytes=24 << 20),
    )(core[None], own, other, gate_weight, up_weight)


def down(core, hidden, down_weight, got, tile):
    slots, units = hidden.shape
    half = got.shape[1]

    def kernel(core_ref, hidden_ref, weight_ref, got_ref, out_ref):
        pair = jnp.dot(hidden_ref[...], weight_ref[...], preferred_element_type=F32)
        pair = (pair + got_ref[...].astype(F32)).astype(BF)
        for i in range(half // tile):
            columns = pair[:, i * tile : (i + 1) * tile]
            if i < Y:
                out_ref[i, :slots] = columns
            else:
                j = 2 * (i - Y)
                out_ref[j, slots:] = columns[: slots // 2]
                out_ref[j + 1, slots:] = columns[slots // 2 :]

    return pl.pallas_call(
        kernel,
        out_shape=jax.ShapeDtypeStruct((Y, slots + slots // 2, tile), BF),
        grid_spec=pltpu.PrefetchScalarGridSpec(
            num_scalar_prefetch=1,
            grid=(1,),
            in_specs=[
                pl.BlockSpec((slots, units), lambda i, core: (0, 0)),
                pl.BlockSpec((units, half), lambda i, core: (0, core[0])),
                pl.BlockSpec((slots, half), lambda i, core: (0, 0)),
            ],
            out_specs=pl.BlockSpec((Y, slots + slots // 2, tile), lambda i, core: (0, 0, 0)),
        ),
        compiler_params=pltpu.CompilerParams(vmem_limit_bytes=16 << 20),
    )(core[None], hidden, down_weight, got)


def join(mine):
    count, rows, block = mine.shape
    tile = block // 2
    tiles = Y + Y // 2

    def kernel(in_ref, out_ref):
        for c in range(C):
            for y in range(Y):
                to = (c * tiles + y) * tile
                out_ref[:, to : to + tile] = in_ref[y * C + c, :, :tile]
            for k in range(Y // 2):
                to = (c * tiles + Y + k) * tile
                a, b = 2 * k * C + c, (2 * k + 1) * C + c
                out_ref[:, to : to + tile] = in_ref[a, :, tile:] + in_ref[b, :, tile:]

    return pl.pallas_call(
        kernel, out_shape=jax.ShapeDtypeStruct((rows, C * tiles * tile), BF)
    )(mine)


def shards(tokens, counts, gate_weight, up_weight, down_weight):
    rows, width = tokens.shape
    hidden_units = gate_weight.shape[1]
    nz = lax.axis_size("z")
    core = lax.axis_index("c")

    near = exchange(cut(tokens), ("y", "c")).reshape(Y * C * rows, -1)
    by_z = exchange(jnp.broadcast_to(near[None], (nz,) + near.shape), "z")

    own = exchange(compact(core, counts, by_z.reshape(nz * Y * C * rows, -1)), "y")
    other = swap(own)

    partial = gate_up(core, own, other, gate_weight, up_weight).astype(jnp.float16)
    parts = lax.all_gather(partial, "gx", axis=0, tiled=False)
    sums = jnp.sum(parts.astype(F32), axis=0) * (1.0 / SCALE)
    hidden = (jax.nn.silu(sums[:, :hidden_units]) * sums[:, hidden_units:]).astype(BF)

    half = width // C
    w_other = lax.dynamic_slice_in_dim(down_weight, (1 - core) * half, half, 1)
    away = jnp.dot(hidden, w_other, preferred_element_type=F32).astype(BF)
    tile = half // Y * 2 // 3
    pieces = down(core, hidden, down_weight, swap(away), tile)

    parity = lax.axis_index("y") % 2
    padded = spread(parity, counts, exchange(pieces, "y")).reshape(nz, Y * C * rows, 2 * tile)
    summed = jnp.sum(exchange(padded, "z").astype(F32), axis=0).astype(BF)
    mine = exchange(summed.reshape(Y * C, rows, 2 * tile), ("y", "c"))
    return join(mine)


def solution(mesh):
    gx, yz = mesh.shape["gx"], mesh.shape["yz"]
    fine = Mesh(mesh.devices.reshape(gx, yz // (Y * C), Y, C), ("gx", "z", "y", "c"))
    line = ("z", "y", "c")
    placed = (P(line, "gx"), P(), P("gx", line), P("gx", line), P(line, "gx"))
    return jax.shard_map(
        shards, mesh=fine, in_specs=placed, out_specs=P(line, "gx"), check_vma=False
    )
```

```python
import jax
import jax.numpy as jnp
from jax import lax
from jax.experimental import pallas as pl
from jax.experimental.pallas import tpu as pltpu
from jax.sharding import Mesh, PartitionSpec as P

GROUP_ROWS = 8
VALID = 192
Y = 8
C = 2
BF = jnp.bfloat16
F32 = jnp.float32
SCALE = 32.0
OVER_ROWS = (((0,), (0,)), ((), ()))


def exchange(x, axis):
    return lax.all_to_all(x, axis, split_axis=0, concat_axis=0, tiled=False)


def swap(x):
    return lax.ppermute(x, "c", [(0, 1), (1, 0)])


def whole(shape):
    return pl.BlockSpec(shape, lambda *_: (0,) * len(shape))


def gate_up(core, own, other, gate_weight, up_weight):
    units = gate_weight.shape[1]
    tile = own.shape[2]
    steps = 3
    chunk = gate_weight.shape[0] // steps

    def kernel(core_ref, own_ref, other_ref, gate_ref, up_ref, out_ref):
        step = pl.program_id(0)
        first = core_ref[0] == 0

        def both(y):
            a, b = own_ref[y], other_ref[y]
            return jnp.where(first, a, b), jnp.where(first, b, a)

        def add(parts, start):
            gate = jnp.zeros((VALID, units), F32)
            up = jnp.zeros((VALID, units), F32)
            for i, x in enumerate(parts):
                depth = pl.ds(i * 2 * tile, 2 * tile)
                gate += jnp.dot(x, gate_ref[depth, :], preferred_element_type=F32)
                up += jnp.dot(x, up_ref[depth, :], preferred_element_type=F32)
            if start:
                out_ref[:, :units] = gate * SCALE
                out_ref[:, units:] = up * SCALE
            else:
                out_ref[:, :units] += gate * SCALE
                out_ref[:, units:] += up * SCALE

        def firsts(start):
            parts = []
            for y in range(start, start + Y // 2):
                a, b = both(y)
                parts.append(jnp.concatenate((a[:VALID], b[:VALID]), axis=1))
            return parts

        def seconds():
            parts = []
            for y in range(0, Y, 2):
                pair = [jnp.concatenate((a[VALID:], b[VALID:]), axis=0) for a, b in (both(y), both(y + 1))]
                parts.append(jnp.concatenate(pair, axis=1))
            return parts

        @pl.when(step == 0)
        def _():
            add(firsts(0), True)

        @pl.when(step == 1)
        def _():
            add(firsts(Y // 2), False)

        @pl.when(step == 2)
        def _():
            add(seconds(), False)

    weights = pl.BlockSpec((chunk, units), lambda i, core: (i, 0))
    return pl.pallas_call(
        kernel,
        out_shape=jax.ShapeDtypeStruct((VALID, 2 * units), F32),
        grid_spec=pltpu.PrefetchScalarGridSpec(
            num_scalar_prefetch=1,
            grid=(steps,),
            in_specs=[whole(own.shape), whole(own.shape), weights, weights],
            out_specs=whole((VALID, 2 * units)),
        ),
        compiler_params=pltpu.CompilerParams(vmem_limit_bytes=24 << 20),
    )(core[None], own, other, gate_weight, up_weight)


def down(core, hidden, down_weight, got, tile):
    slots, units = hidden.shape
    half = got.shape[1]

    def kernel(core_ref, hidden_ref, weight_ref, got_ref, out_ref):
        pair = jnp.dot(hidden_ref[...], weight_ref[...], preferred_element_type=F32)
        pair = (pair + got_ref[...].astype(F32)).astype(BF)
        for i in range(half // tile):
            columns = pair[:, i * tile : (i + 1) * tile]
            if i < Y:
                out_ref[i, :slots] = columns
            else:
                j = 2 * (i - Y)
                out_ref[j, slots:] = columns[: slots // 2]
                out_ref[j + 1, slots:] = columns[slots // 2 :]

    return pl.pallas_call(
        kernel,
        out_shape=jax.ShapeDtypeStruct((Y, slots + slots // 2, tile), BF),
        grid_spec=pltpu.PrefetchScalarGridSpec(
            num_scalar_prefetch=1,
            grid=(1,),
            in_specs=[
                pl.BlockSpec((slots, units), lambda i, core: (0, 0)),
                pl.BlockSpec((units, half), lambda i, core: (0, core[0])),
                pl.BlockSpec((slots, half), lambda i, core: (0, 0)),
            ],
            out_specs=pl.BlockSpec((Y, slots + slots // 2, tile), lambda i, core: (0, 0, 0)),
        ),
        compiler_params=pltpu.CompilerParams(vmem_limit_bytes=16 << 20),
    )(core[None], hidden, down_weight, got)


def one_hot(starts, ends, columns, shift):
    shape = (starts.shape[0], GROUP_ROWS, columns)
    row = lax.broadcasted_iota(jnp.int32, shape, 1)
    place = lax.broadcasted_iota(jnp.int32, shape, 2) + shift
    hit = (place - row == starts[:, None, None]) & (place < ends[:, None, None])
    return hit.astype(BF).reshape(-1, columns)


def shards(tokens, counts, gate_weight, up_weight, down_weight):
    rows, width = tokens.shape
    hidden_units = gate_weight.shape[1]
    nz = lax.axis_size("z")
    near = Y * C * rows
    tile = width // (Y * C + Y)
    half_rows = VALID // 2

    core = lax.axis_index("c")
    shift = lax.axis_index("y") % 2 * half_rows
    w_start = (1 - core) * (width // C)
    half_start = core * half_rows
    groups = jnp.arange(counts.shape[0], dtype=jnp.int32)
    starts = jnp.sum(jnp.where(groups[None, :] < groups[:, None], counts[None, :], 0), axis=1)
    ends = jnp.sum(jnp.where(groups[None, :] <= groups[:, None], counts[None, :], 0), axis=1)
    hot = one_hot(starts, ends, VALID, 0)
    hot_half = one_hot(starts, ends, half_rows, shift)
    tokens, hot, hot_half, core, w_start, half_start = lax.optimization_barrier(
        (tokens, hot, hot_half, core, w_start, half_start)
    )

    tiles = tokens.reshape(rows, width // tile, tile).transpose(1, 0, 2)
    seconds = jnp.repeat(tiles[Y * C :], C, axis=0)
    cut = jnp.stack((tiles[: Y * C], seconds), axis=1)
    got = exchange(cut, ("y", "c")).transpose(0, 2, 1, 3).reshape(near, 2 * tile)
    by_z = exchange(jnp.broadcast_to(got[None], (nz,) + got.shape), "z")
    by_z = by_z.reshape(nz * near, 2 * tile)

    valid = lax.dot_general(hot, by_z, OVER_ROWS, preferred_element_type=F32).astype(BF)
    second = lax.dynamic_slice(
        valid, (half_start, tile), (half_rows, tile), allow_negative_indices=False
    )
    block = jnp.concatenate((valid[:, :tile], second), axis=0)
    own = exchange(jnp.broadcast_to(block[None], (Y,) + block.shape), "y")
    other = swap(own)

    partial = gate_up(core, own, other, gate_weight, up_weight).astype(jnp.float16)
    parts = lax.all_gather(partial, "gx", axis=0, tiled=False)
    sums = jnp.sum(parts.astype(F32), axis=0) * (1.0 / SCALE)
    hidden = (jax.nn.silu(sums[:, :hidden_units]) * sums[:, hidden_units:]).astype(BF)

    w_other = lax.dynamic_slice(
        down_weight, (0, w_start), (hidden_units, width // C), allow_negative_indices=False
    )
    away = jnp.dot(hidden, w_other, preferred_element_type=F32).astype(BF)
    pieces = down(core, hidden, down_weight, swap(away), tile)
    column = jnp.sum(exchange(pieces, "y").astype(F32), axis=0).astype(BF)

    padded = jnp.concatenate(
        (
            jnp.dot(hot, column[:VALID], preferred_element_type=F32).astype(BF),
            jnp.dot(hot_half, column[VALID:], preferred_element_type=F32).astype(BF),
        ),
        axis=1,
    ).reshape(nz, near, 2 * tile)
    summed = jnp.sum(exchange(padded, "z").astype(F32), axis=0).astype(BF)
    home = summed.reshape(Y * C, rows, 2, tile).transpose(0, 2, 1, 3)
    mine = exchange(home, ("y", "c")).reshape(Y, C, 2, rows, tile)
    firsts = mine[:, :, 0].transpose(1, 0, 2, 3)
    pairs = mine[:, :, 1].reshape(Y // 2, 2, C, rows, tile)
    seconds = (pairs[:, 0] + pairs[:, 1]).transpose(1, 0, 2, 3)
    out = jnp.concatenate((firsts, seconds), axis=1).reshape(width // tile, rows, tile)
    return out.transpose(1, 0, 2).reshape(rows, width)


def solution(mesh):
    gx, yz = mesh.shape["gx"], mesh.shape["yz"]
    fine = Mesh(mesh.devices.reshape(gx, yz // (Y * C), Y, C), ("gx", "z", "y", "c"))
    line = ("z", "y", "c")
    placed = (P(line, "gx"), P(), P("gx", line), P("gx", line), P(line, "gx"))
    return jax.shard_map(
        shards, mesh=fine, in_specs=placed, out_specs=P(line, "gx"), check_vma=False
    )
```

```python
import jax
import jax.numpy as jnp
from jax import lax
from jax.experimental import pallas as pl
from jax.experimental.pallas import tpu as pltpu
from jax.sharding import Mesh, PartitionSpec as P

GROUP_ROWS = 8
VALID = 192
Y = 8
C = 2
BF = jnp.bfloat16
F32 = jnp.float32
SCALE = 32.0
OVER_ROWS = (((0,), (0,)), ((), ()))


def exchange(x, axis):
    return lax.all_to_all(x, axis, split_axis=0, concat_axis=0, tiled=False)


def swap(x):
    return lax.ppermute(x, "c", [(0, 1), (1, 0)])


def whole(shape):
    return pl.BlockSpec(shape, lambda *_: (0,) * len(shape))


def gate_up(core, own, other, gate_weight, up_weight):
    units = gate_weight.shape[1]
    tile = own.shape[2]
    steps = 3
    chunk = gate_weight.shape[0] // steps

    def kernel(core_ref, own_ref, other_ref, gate_ref, up_ref, out_ref):
        step = pl.program_id(0)
        first = core_ref[0] == 0

        def both(y):
            a, b = own_ref[y], other_ref[y]
            return jnp.where(first, a, b), jnp.where(first, b, a)

        def add(parts, start):
            gate = jnp.zeros((VALID, units), F32)
            up = jnp.zeros((VALID, units), F32)
            for i, x in enumerate(parts):
                depth = pl.ds(i * 2 * tile, 2 * tile)
                gate += jnp.dot(x, gate_ref[depth, :], preferred_element_type=F32)
                up += jnp.dot(x, up_ref[depth, :], preferred_element_type=F32)
            if start:
                out_ref[:, :units] = gate * SCALE
                out_ref[:, units:] = up * SCALE
            else:
                out_ref[:, :units] += gate * SCALE
                out_ref[:, units:] += up * SCALE

        def firsts(start):
            parts = []
            for y in range(start, start + Y // 2):
                a, b = both(y)
                parts.append(jnp.concatenate((a[:VALID], b[:VALID]), axis=1))
            return parts

        def seconds():
            parts = []
            for y in range(0, Y, 2):
                pair = [jnp.concatenate((a[VALID:], b[VALID:]), axis=0) for a, b in (both(y), both(y + 1))]
                parts.append(jnp.concatenate(pair, axis=1))
            return parts

        @pl.when(step == 0)
        def _():
            add(firsts(0), True)

        @pl.when(step == 1)
        def _():
            add(firsts(Y // 2), False)

        @pl.when(step == 2)
        def _():
            add(seconds(), False)

    weights = pl.BlockSpec((chunk, units), lambda i, core: (i, 0))
    return pl.pallas_call(
        kernel,
        out_shape=jax.ShapeDtypeStruct((VALID, 2 * units), F32),
        grid_spec=pltpu.PrefetchScalarGridSpec(
            num_scalar_prefetch=1,
            grid=(steps,),
            in_specs=[whole(own.shape), whole(own.shape), weights, weights],
            out_specs=whole((VALID, 2 * units)),
        ),
        compiler_params=pltpu.CompilerParams(vmem_limit_bytes=24 << 20),
    )(core[None], own, other, gate_weight, up_weight)


def down(core, hidden, down_weight, got, tile):
    slots, units = hidden.shape
    half = got.shape[1]

    def kernel(core_ref, hidden_ref, weight_ref, got_ref, out_ref):
        pair = jnp.dot(hidden_ref[...], weight_ref[...], preferred_element_type=F32)
        pair = (pair + got_ref[...].astype(F32)).astype(BF)
        for i in range(half // tile):
            columns = pair[:, i * tile : (i + 1) * tile]
            if i < Y:
                out_ref[i, :slots] = columns
            else:
                j = 2 * (i - Y)
                out_ref[j, slots:] = columns[: slots // 2]
                out_ref[j + 1, slots:] = columns[slots // 2 :]

    return pl.pallas_call(
        kernel,
        out_shape=jax.ShapeDtypeStruct((Y, slots + slots // 2, tile), BF),
        grid_spec=pltpu.PrefetchScalarGridSpec(
            num_scalar_prefetch=1,
            grid=(1,),
            in_specs=[
                pl.BlockSpec((slots, units), lambda i, core: (0, 0)),
                pl.BlockSpec((units, half), lambda i, core: (0, core[0])),
                pl.BlockSpec((slots, half), lambda i, core: (0, 0)),
            ],
            out_specs=pl.BlockSpec((Y, slots + slots // 2, tile), lambda i, core: (0, 0, 0)),
        ),
        compiler_params=pltpu.CompilerParams(vmem_limit_bytes=16 << 20),
    )(core[None], hidden, down_weight, got)


def one_hot(starts, ends, columns, shift):
    shape = (starts.shape[0], GROUP_ROWS, columns)
    row = lax.broadcasted_iota(jnp.int32, shape, 1)
    place = lax.broadcasted_iota(jnp.int32, shape, 2) + shift
    hit = (place - row == starts[:, None, None]) & (place < ends[:, None, None])
    return hit.astype(BF).reshape(-1, columns)


def shards(tokens, counts, gate_weight, up_weight, down_weight):
    rows, width = tokens.shape
    hidden_units = gate_weight.shape[1]
    nz = lax.axis_size("z")
    near = Y * C * rows
    tile = width // (Y * C + Y)
    half_rows = VALID // 2

    core = lax.axis_index("c")
    shift = lax.axis_index("y") % 2 * half_rows
    w_start = (1 - core) * (width // C)
    half_start = core * half_rows
    groups = jnp.arange(counts.shape[0], dtype=jnp.int32)
    starts = jnp.sum(jnp.where(groups[None, :] < groups[:, None], counts[None, :], 0), axis=1)
    ends = jnp.sum(jnp.where(groups[None, :] <= groups[:, None], counts[None, :], 0), axis=1)
    hot = one_hot(starts, ends, VALID, 0)
    hot_half = one_hot(starts, ends, half_rows, shift)

    tiles = tokens.reshape(rows, width // tile, tile).transpose(1, 0, 2)
    seconds = jnp.repeat(tiles[Y * C :], C, axis=0)
    cut = jnp.stack((tiles[: Y * C], seconds), axis=1)
    got = exchange(cut, ("y", "c"))
    got, hot, hot_half, core, w_start, half_start = lax.optimization_barrier(
        (got, hot, hot_half, core, w_start, half_start)
    )
    got = got.transpose(0, 2, 1, 3).reshape(near, 2 * tile)
    by_z = exchange(jnp.broadcast_to(got[None], (nz,) + got.shape), "z")
    by_z = by_z.reshape(nz * near, 2 * tile)

    valid = lax.dot_general(hot, by_z, OVER_ROWS, preferred_element_type=F32).astype(BF)
    second = lax.dynamic_slice(
        valid, (half_start, tile), (half_rows, tile), allow_negative_indices=False
    )
    block = jnp.concatenate((valid[:, :tile], second), axis=0)
    own = exchange(jnp.broadcast_to(block[None], (Y,) + block.shape), "y")
    other = swap(own)

    partial = gate_up(core, own, other, gate_weight, up_weight).astype(jnp.float16)
    parts = lax.all_gather(partial, "gx", axis=0, tiled=False)
    sums = jnp.sum(parts.astype(F32), axis=0) * (1.0 / SCALE)
    hidden = (jax.nn.silu(sums[:, :hidden_units]) * sums[:, hidden_units:]).astype(BF)

    w_other = lax.dynamic_slice(
        down_weight, (0, w_start), (hidden_units, width // C), allow_negative_indices=False
    )
    away = jnp.dot(hidden, w_other, preferred_element_type=F32).astype(BF)
    pieces = down(core, hidden, down_weight, swap(away), tile)
    column = jnp.sum(exchange(pieces, "y").astype(F32), axis=0).astype(BF)

    padded = jnp.concatenate(
        (
            jnp.dot(hot, column[:VALID], preferred_element_type=F32).astype(BF),
            jnp.dot(hot_half, column[VALID:], preferred_element_type=F32).astype(BF),
        ),
        axis=1,
    ).reshape(nz, near, 2 * tile)
    summed = jnp.sum(exchange(padded, "z").astype(F32), axis=0).astype(BF)
    home = summed.reshape(Y * C, rows, 2, tile).transpose(0, 2, 1, 3)
    mine = exchange(home, ("y", "c")).reshape(Y, C, 2, rows, tile)
    firsts = mine[:, :, 0].transpose(1, 0, 2, 3)
    pairs = mine[:, :, 1].reshape(Y // 2, 2, C, rows, tile)
    seconds = (pairs[:, 0] + pairs[:, 1]).transpose(1, 0, 2, 3)
    out = jnp.concatenate((firsts, seconds), axis=1).reshape(width // tile, rows, tile)
    return out.transpose(1, 0, 2).reshape(rows, width)


def solution(mesh):
    gx, yz = mesh.shape["gx"], mesh.shape["yz"]
    fine = Mesh(mesh.devices.reshape(gx, yz // (Y * C), Y, C), ("gx", "z", "y", "c"))
    line = ("z", "y", "c")
    placed = (P(line, "gx"), P(), P("gx", line), P("gx", line), P(line, "gx"))
    return jax.shard_map(
        shards, mesh=fine, in_specs=placed, out_specs=P(line, "gx"), check_vma=False
    )
```
